128 devices in a mesh: fsdp: 16 (over x_hi, z, core), tp: 8 (over x_lo, y).
Axes of the slice: x: 4 (x_hi: 2, x_lo: 2; x = x_hi * 2 + x_lo), y: 4, z: 4, core: 2. Of those that a mesh axis runs over, the one named last changes fastest.
Arguments:
- hidden: bfloat16 [6144, 7168], P('fsdp'), may hold values from -72 to 72
- w_query: bfloat16 [7168, 4096], P('fsdp', 'tp'), may hold values from -0.0625 to 0.0625
- w_key: bfloat16 [7168, 1024], P('fsdp', 'tp'), may hold values from -0.0625 to 0.0625
- w_value: bfloat16 [7168, 1024], P('fsdp', 'tp'), may hold values from -0.0625 to 0.0625
- w_out: bfloat16 [4096, 7168], P('tp', 'fsdp'), may hold values from -0.09375 to 0.09375
- exp_query: int32 [56, 32], replicated, may hold values from -1 to 1
- exp_key: int32 [56, 8], replicated, may hold values from -1 to 1
- exp_value: int32 [56, 8], replicated, may hold values from -1 to 1
- exp_out: int32 [32, 56], replicated, may hold values from -1 to 1
- owner: int32 [16], replicated, may hold values from 0 to 15, each once
Outputs:
- attended: bfloat16 [6144, 7168], P('fsdp', 'tp')
The draws below stay inside these ranges and needn't reach their ends.
Inputs may be any that keep to these rules, and one draw needn't show every extreme that they name: Trainer shard i holds logical slab owner[i]; every slab is held once.
All inputs are finite; a program needn't handle non-finite values.
Results may differ from the reference program's by a relative error of at most 0.038.
Values may be sent and summed in bfloat16 or wider, within the bound.
No kernel may reach another device: no remote copies, remote signals or barrier semaphores. Data moves between devices by JAX's collectives and lax.ppermute only.
A program may use at most 128 MiB of HBM per device.

```python
import math
import jax
import jax.numpy as jnp
from jax import lax

D = 7168
HQ = 32
HK = 8
HD = 128
BLOCK = 128
TOKENS = 6144
QW = 4096
KW = 1024
N_FSDP = 16
N_TP = 8


def draw_hidden(key, part):
    first = jax.random.fold_in(jax.random.fold_in(key, 17), 0)
    values = jnp.clip(jax.random.normal(first, (TOKENS, D), jnp.float32), -6.0, 6.0)
    return values.astype(jnp.bfloat16)


def with_ends(entries, stream_key, least, largest):
    longest = entries.shape.index(max(entries.shape))
    spots = []
    for shift in (0, 1):
        where = [jax.random.randint(jax.random.fold_in(stream_key, axis), (), 0, length) for axis, length in enumerate(entries.shape)]
        where[longest] = (where[longest] + shift) % entries.shape[longest]
        spots.append(tuple(where))
    return entries.at[spots[0]].set(least).at[spots[1]].set(largest)


def level_of(key, extent, cuts, smallest, top_value):
    factor_of, own = 1.0, jax.random.fold_in(key, 6)
    for axis_at, blocks in cuts:
        heights = jnp.exp(jax.random.uniform(jax.random.fold_in(own, axis_at), (blocks,), jnp.float32, smallest / len(cuts), top_value / len(cuts)))
        factor_of = factor_of * jnp.repeat(heights, extent[axis_at] // blocks).reshape([-1 if axis == axis_at else 1 for axis in range(len(extent))])
    return factor_of


def scatter_about(key, dims, spread, reach, pieces=(), held_as=jnp.bfloat16):
    entries = spread * jax.random.normal(key, dims, jnp.float32)
    if pieces:
        entries = entries * level_of(key, dims, pieces, -0.22, 0.18)
    return jnp.clip(entries, -reach, reach).astype(held_as)


def setup_inputs(seed: int = 0) -> dict:
    streams_of = jax.random.split(jax.random.key(seed), 11)
    hidden = draw_hidden(jax.random.fold_in(streams_of[10], 71), 0)
    w_query = scatter_about(streams_of[1], (D, QW), D ** -0.5, 0.0625, ((0, 16), (1, 8)))
    w_key = scatter_about(streams_of[2], (D, KW), D ** -0.5, 0.0625, ((0, 16), (1, 8)))
    w_value = scatter_about(streams_of[3], (D, KW), D ** -0.5, 0.0625, ((0, 16), (1, 8)))
    w_out = scatter_about(streams_of[4], (QW, D), QW ** -0.5, 0.09375, ((0, 8), (1, 16)))
    exp_query = with_ends(jax.random.randint(streams_of[5], (D // BLOCK, QW // BLOCK), -1, 2), jax.random.fold_in(streams_of[5], 1), -1, 1).astype(jnp.int32)
    exp_key = with_ends(jax.random.randint(streams_of[6], (D // BLOCK, KW // BLOCK), -1, 2), jax.random.fold_in(streams_of[6], 1), -1, 1).astype(jnp.int32)
    exp_value = with_ends(jax.random.randint(streams_of[7], (D // BLOCK, KW // BLOCK), -1, 2), jax.random.fold_in(streams_of[7], 1), -1, 1).astype(jnp.int32)
    exp_out = with_ends(jax.random.randint(streams_of[8], (QW // BLOCK, D // BLOCK), -1, 2), jax.random.fold_in(streams_of[8], 1), -1, 1).astype(jnp.int32)
    owner = jax.random.permutation(streams_of[9], N_FSDP).astype(jnp.int32)
    return dict(hidden=hidden, w_query=w_query, w_key=w_key, w_value=w_value, w_out=w_out, exp_query=exp_query, exp_key=exp_key, exp_value=exp_value, exp_out=exp_out, owner=owner)


neg_large = -1e+30

def dequantize(weight, exponents):
    block_size = weight.shape[0] // exponents.shape[0]
    factor = jnp.exp2(exponents.astype(jnp.float32))
    factor = jnp.repeat(jnp.repeat(factor, block_size, axis=0), block_size, axis=1)
    return (weight.astype(jnp.float32) * factor).astype(jnp.bfloat16)

def reference(hidden, w_query, w_key, w_value, w_out, exp_query, exp_key, exp_value, exp_out, owner):
    slab_rows = D // N_FSDP
    inverse = jnp.argsort(owner).astype(jnp.int32)

    def rows_logical(weight):
        shaped = weight.reshape(N_FSDP, slab_rows, weight.shape[1])
        return jnp.take(shaped, inverse, axis=0).reshape(weight.shape)

    def cols_logical(weight):
        shaped = weight.reshape(weight.shape[0], N_FSDP, slab_rows)
        return jnp.take(shaped, inverse, axis=1).reshape(weight.shape)
    query_w = dequantize(rows_logical(w_query), exp_query)
    key_w = dequantize(rows_logical(w_key), exp_key)
    value_w = dequantize(rows_logical(w_value), exp_value)
    out_w = dequantize(cols_logical(w_out), exp_out)
    query = jnp.dot(hidden, query_w, preferred_element_type=jnp.float32).astype(jnp.bfloat16)
    key_all = jnp.dot(hidden, key_w, preferred_element_type=jnp.float32).astype(jnp.bfloat16)
    value_all = jnp.dot(hidden, value_w, preferred_element_type=jnp.float32).astype(jnp.bfloat16)
    tokens = hidden.shape[0]
    group_size = HQ // HK
    query_heads = query.reshape(tokens, HQ, HD).transpose(1, 0, 2)
    key_heads = key_all.reshape(tokens, HK, HD).transpose(1, 0, 2)
    value_heads = value_all.reshape(tokens, HK, HD).transpose(1, 0, 2)
    position = jnp.arange(tokens, dtype=jnp.int32)
    causal = position[:, None] >= position[None, :]
    inv_root = 1.0 / math.sqrt(HD)

    def one_head(head_index):
        query_one = query_heads[head_index]
        key_one = key_heads[head_index // group_size]
        value_one = value_heads[head_index // group_size]
        scores = jnp.dot(query_one, key_one.T, preferred_element_type=jnp.float32) * inv_root
        scores = jnp.where(causal, scores, neg_large)
        row_top = lax.optimization_barrier(jnp.max(scores, axis=1, keepdims=True))
        weights = jnp.where(causal, jnp.exp(scores - row_top), 0.0)
        row_total = lax.optimization_barrier(jnp.sum(weights, axis=1, keepdims=True))
        mixed_sum = jnp.dot(weights.astype(jnp.bfloat16), value_one, preferred_element_type=jnp.float32)
        return (mixed_sum / row_total).astype(jnp.bfloat16)
    context = lax.map(one_head, jnp.arange(HQ, dtype=jnp.int32))
    context = context.transpose(1, 0, 2).reshape(tokens, HQ * HD)
    rows_tp = HQ * HD // N_TP
    attended = jnp.zeros((tokens, D), jnp.float32)
    for tp_rank in range(N_TP):
        part_sum = jnp.dot(context[:, tp_rank * rows_tp:(tp_rank + 1) * rows_tp], out_w[tp_rank * rows_tp:(tp_rank + 1) * rows_tp], preferred_element_type=jnp.float32)
        rounded = lax.optimization_barrier(part_sum.astype(jnp.bfloat16))
        attended = attended + rounded.astype(jnp.float32)
    return attended.astype(jnp.bfloat16)
```

```python
import functools
import math

import jax
import jax.numpy as jnp
from jax import lax
from jax.experimental import pallas as pl
from jax.experimental.pallas import tpu as pltpu
from jax.sharding import Mesh
from jax.sharding import PartitionSpec as P

D = 7168
TOK = 384
SLAB = 448
OUTW = 896
NEG = -1e30
BF = jnp.bfloat16
F32 = jnp.float32
FS = ("x_hi", "z", "core")
TP = ("x_lo", "y")
VM = pltpu.MemorySpace.VMEM
SM = pltpu.MemorySpace.SMEM
REL = ((0, 0), (0, 3), (0, 1), (1, 0), (1, 3), (0, 2), (1, 1), (1, 2))
NT = (((1,), (1,)), ((), ()))


def params(mib):
    return pltpu.CompilerParams(vmem_limit_bytes=mib << 20)


def cost(flops, nbytes, trans=0):
    return pl.CostEstimate(flops=flops, bytes_accessed=nbytes, transcendentals=trans)


def fsdp_pos():
    return (lax.axis_index("x_hi") * 4 + lax.axis_index("z")) * 2 + lax.axis_index("core")


def tp_pos():
    return lax.axis_index("x_lo") * 4 + lax.axis_index("y")


def fsdp_of(rel, other_core):
    dx, dz = rel
    hi = lax.axis_index("x_hi")
    core = lax.axis_index("core")
    hi = 1 - hi if dx else hi
    core = 1 - core if other_core else core
    return (hi * 4 + lax.rem(lax.axis_index("z") + dz, 4)) * 2 + core


def tp_of(rel):
    dx, dy = rel
    lo = lax.axis_index("x_lo")
    lo = 1 - lo if dx else lo
    return lo * 4 + lax.rem(lax.axis_index("y") + dy, 4)


def shift(x, axis, by):
    return lax.ppermute(x, axis, [(i, (i + by) % 4) for i in range(4)])


def swap(x, axis):
    return lax.ppermute(x, axis, [(0, 1), (1, 0)])


def scale_kernel(owner, eq, ek, ev, eo, wq, wk, wv, wo, kv_out, q_out, wo_out):
    slab = owner[fsdp_pos()]
    t = tp_pos()

    def factor(e):
        return jnp.where(e > 0, 2.0, jnp.where(e < 0, 0.5, 1.0)).astype(F32)

    def scaled(x, e):
        return (x.astype(F32) * factor(e)).astype(BF)

    turned = [wo[k * 128 : (k + 1) * 128, :].T for k in range(4)]
    for j in range(7):
        rows = slice(j * 64, (j + 1) * 64)
        block = (slab * 7 + j) // 2
        kv_out[rows, 0:128] = scaled(wk[rows, :], ek[block, t])
        kv_out[rows, 128:256] = scaled(wv[rows, :], ev[block, t])
        for h in range(4):
            cols = slice(h * 128, (h + 1) * 128)
            q_out[rows, cols] = scaled(wq[rows, cols], eq[block, t * 4 + h])
            wo_out[rows, cols] = scaled(turned[h][rows, :], eo[t * 4 + h, block])


def scale(owner, eq, ek, ev, eo, wq, wk, wv, wo):
    return pl.pallas_call(
        scale_kernel,
        in_specs=[pl.BlockSpec(memory_space=SM)] * 5 + [pl.BlockSpec(memory_space=VM)] * 4,
        out_specs=[pl.BlockSpec(memory_space=VM)] * 3,
        out_shape=[
            jax.ShapeDtypeStruct((SLAB, 256), BF),
            jax.ShapeDtypeStruct((SLAB, 512), BF),
            jax.ShapeDtypeStruct((SLAB, 512), BF),
        ],
        compiler_params=params(24),
        cost_estimate=cost(1 << 20, 3 << 20),
        name="scale",
    )(owner, eq, ek, ev, eo, wq, wk, wv, wo)


def proj_kernel(split, owner, hid, *refs):
    n_w = 2 if split else 1
    weights = refs[:n_w]
    out, held, acc, sems = refs[n_w:]
    step = pl.program_id(0)

    @pl.when(step == 0)
    def _():
        copies = []
        for p in range(16):
            if split:
                src = weights[p // 8].at[pl.ds((p % 8) * SLAB, SLAB), :]
                slab = owner[fsdp_of(REL[p % 8], p >= 8)]
            else:
                src = weights[0].at[pl.ds(p * SLAB, SLAB), :]
                slab = owner[p]
            at = pl.multiple_of(slab * SLAB, 64)
            copy = pltpu.make_async_copy(src, held.at[pl.ds(at, SLAB), :], sems.at[p])
            copy.start()
            copies.append(copy)
        for copy in copies:
            copy.wait()
        acc[...] = jnp.zeros_like(acc)

    at = pl.multiple_of(step * 1024, 1024)
    acc[...] += jnp.dot(hid[...], held[pl.ds(at, 1024), :], preferred_element_type=F32)

    @pl.when(step == 6)
    def _():
        out[...] = acc[...].astype(BF)


def proj(owner, hidden, weights, name):
    n = weights[0].shape[1]
    split = len(weights) == 2
    return pl.pallas_call(
        functools.partial(proj_kernel, split),
        grid=(7,),
        in_specs=[
            pl.BlockSpec(memory_space=SM),
            pl.BlockSpec((TOK, 1024), lambda k: (0, k)),
            *[pl.BlockSpec(memory_space=pl.ANY)] * len(weights),
        ],
        out_specs=pl.BlockSpec((TOK, n), lambda k: (0, 0)),
        out_shape=jax.ShapeDtypeStruct((TOK, n), BF),
        scratch_shapes=[
            pltpu.VMEM((D, n), BF),
            pltpu.VMEM((TOK, n), F32),
            pltpu.SemaphoreType.DMA((16,)),
        ],
        compiler_params=params(24),
        cost_estimate=cost(2 * TOK * D * n, 2 * D * (n + TOK)),
        name=name,
    )(owner, hidden, *weights)


def attend_kernel(q, kv, out, top, acc):
    f = fsdp_pos()
    c = math.log2(math.e) / math.sqrt(128)
    ones = jnp.ones((TOK, 128), BF)

    def block(j):
        at = pl.multiple_of(j * TOK, TOK)
        keys = kv[pl.ds(at, TOK), 0:128]
        values = jnp.concatenate([kv[pl.ds(at, TOK), 128:256], ones], axis=1)
        return keys, values

    keys, values = block(f)
    row = lax.broadcasted_iota(jnp.int32, (TOK, TOK), 0)
    col = lax.broadcasted_iota(jnp.int32, (TOK, TOK), 1)
    for h in range(4):
        s = lax.dot_general(q[:, h * 128 : (h + 1) * 128], keys, NT, preferred_element_type=F32) * c
        s = jnp.where(row >= col, s, NEG)
        m = jnp.max(s, axis=1, keepdims=True)
        w = jnp.exp2(s - m).astype(BF)
        top[h] = jnp.broadcast_to(m, (TOK, 128))
        acc[h] = jnp.dot(w, values, preferred_element_type=F32)

    def earlier(j, carry):
        keys, values = block(j)
        for h in range(4):
            s = lax.dot_general(q[:, h * 128 : (h + 1) * 128], keys, NT, preferred_element_type=F32) * c
            old = top[h][:, 0:1]
            m = jnp.maximum(old, jnp.max(s, axis=1, keepdims=True))
            w = jnp.exp2(s - m).astype(BF)
            top[h] = jnp.broadcast_to(m, (TOK, 128))
            acc[h] = acc[h] * jnp.exp2(old - m) + jnp.dot(w, values, preferred_element_type=F32)
        return carry

    lax.fori_loop(0, f, earlier, 0)
    for h in range(4):
        out[:, h * 128 : (h + 1) * 128] = (acc[h][:, 0:128] / acc[h][:, 128:256]).astype(BF)


def attend(q, kv):
    return pl.pallas_call(
        attend_kernel,
        in_specs=[pl.BlockSpec(memory_space=VM)] * 2,
        out_specs=pl.BlockSpec(memory_space=VM),
        out_shape=jax.ShapeDtypeStruct((TOK, 512), BF),
        scratch_shapes=[pltpu.VMEM((4, TOK, 128), F32), pltpu.VMEM((4, TOK, 256), F32)],
        compiler_params=params(32),
        cost_estimate=cost(4 * 4 * TOK * 6144 * 128, 4 << 20, 4 * TOK * 6144),
        name="attend",
    )(q, kv)


def out_kernel(dests, adds, cuts, n_add, owner, ctx, mine, theirs, *refs):
    addends = refs[:n_add]
    outs = refs[n_add:-2]
    held, sems = refs[-2:]
    slabs = [owner[fsdp_of(REL[p % 8], p >= 8)] for p in range(16)]
    for i, dest in enumerate(dests):
        t = tp_of(dest)
        for p in range(16):

            @pl.when(slabs[p] // 2 == t)
            def _():
                half = lax.rem(slabs[p], 2)
                at = pl.multiple_of(i * OUTW + half * SLAB, 64)
                src = (theirs if p >= 8 else mine).at[pl.ds((p % 8) * SLAB, SLAB), :]
                pltpu.make_async_copy(src, held.at[pl.ds(at, SLAB), :], sems.at[2 * i + half]).start()

    o = 0
    for i in range(len(dests)):
        for half in range(2):
            there = held.at[pl.ds(i * OUTW + half * SLAB, SLAB), :]
            pltpu.make_async_copy(mine.at[pl.ds(0, SLAB), :], there, sems.at[2 * i + half]).wait()
        for r0, r1 in cuts:
            part = lax.dot_general(
                ctx[r0:r1, :], held[i * OUTW : (i + 1) * OUTW, :], NT, preferred_element_type=F32
            )
            for which, a0 in adds[i]:
                rows = addends[which].shape[0]
                lo, hi = max(a0, r0), min(a0 + rows, r1)
                if lo >= hi:
                    continue
                extra = addends[which][lo - a0 : hi - a0, :].astype(F32)
                pieces = []
                if lo > r0:
                    pieces.append(part[: lo - r0, :])
                pieces.append(part[lo - r0 : hi - r0, :] + extra)
                if hi < r1:
                    pieces.append(part[hi - r0 :, :])
                part = jnp.concatenate(pieces, axis=0) if len(pieces) > 1 else pieces[0]
            outs[o][...] = part.astype(BF)
            o += 1


def project_out(owner, ctx, mine, theirs, dests, adds, addends, name, cuts=((0, TOK),)):
    n = len(dests)
    return pl.pallas_call(
        functools.partial(out_kernel, dests, adds, cuts, len(addends)),
        in_specs=[
            pl.BlockSpec(memory_space=SM),
            pl.BlockSpec(memory_space=VM),
            *[pl.BlockSpec(memory_space=pl.ANY)] * 2,
            *[pl.BlockSpec(memory_space=VM)] * len(addends),
        ],
        out_specs=[pl.BlockSpec(memory_space=VM)] * (n * len(cuts)),
        out_shape=[jax.ShapeDtypeStruct((r1 - r0, OUTW), BF) for _ in range(n) for r0, r1 in cuts],
        scratch_shapes=[pltpu.VMEM((n * OUTW, 512), BF), pltpu.SemaphoreType.DMA((2 * n,))],
        compiler_params=params(32),
        cost_estimate=cost(2 * n * TOK * 512 * OUTW, n * (3 << 20)),
        name=name,
    )(owner, ctx, mine, theirs, *addends)


def gather_chips(own):
    a1, a2, a3 = shift(own, "z", 1), shift(own, "z", -1), swap(own, "x_hi")
    b1, b2, b3 = shift(a3, "z", 1), shift(a2, "z", -1), swap(a2, "x_hi")
    rows = own.shape[0]
    t1 = -(-rows // 48) * 16
    t2 = t1 + (rows - t1) // 32 * 16
    c1 = shift(b1[:t1], "z", 1)
    c2 = shift(b3[t1:t2], "z", -1)
    c3 = swap(b2[t2:], "x_hi")
    return jnp.concatenate([own, a1, a2, a3, b1, b2, b3, c1, c2, c3], axis=0)


def body(hidden, w_query, w_key, w_value, w_out, exp_query, exp_key, exp_value, exp_out, owner):
    w_kv, w_q, w_o = scale(owner, exp_query, exp_key, exp_value, exp_out, w_query, w_key, w_value, w_out)
    kv_all = lax.all_gather(w_kv, FS, axis=0, tiled=True)
    q_mine = gather_chips(w_q)
    q_theirs = swap(q_mine, "core")
    kv_here = proj(owner, hidden, [kv_all], "proj_kv")
    kv = lax.all_gather(kv_here, FS, axis=0, tiled=True)
    o_mine = gather_chips(w_o)
    o_theirs = swap(o_mine, "core")
    query = proj(owner, hidden, [q_mine, q_theirs], "proj_q")
    ctx = attend(query, kv)

    out = functools.partial(project_out, owner, ctx, o_mine, o_theirs)
    thirds = ((0, 128), (128, 256), (256, 384))
    p1, p2, p3 = out(((1, 2),), ((),), (), "out_far", cuts=thirds)
    r1, r2, r3 = shift(p1, "y", -1), shift(p2, "y", 1), swap(p3, "x_lo")
    s1, s2, s3 = out(
        ((1, 3), (0, 2), (1, 1)), (((0, 0),), ((1, 256),), ((2, 128),)), (r1, r3, r2), "out_mid"
    )
    u1, u2, u3 = shift(s1, "y", -1), shift(s2, "y", 1), swap(s3, "x_lo")
    v1, v2, v3 = out(
        ((0, 3), (0, 1), (1, 0)), ((), ((0, 0), (1, 0)), ((2, 0),)), (u2, u3, u1), "out_near"
    )
    g1, g2, g3 = shift(v1, "y", -1), shift(v2, "y", 1), swap(v3, "x_lo")
    (result,) = out(((0, 0),), (((0, 0), (1, 0), (2, 0)),), (g1, g2, g3), "out_own")
    return result


def solution(mesh):
    fine = Mesh(mesh.devices.reshape(2, 4, 2, 2, 4), ("x_hi", "z", "core", "x_lo", "y"))
    placed = (
        P(FS, None),
        P(FS, TP),
        P(FS, TP),
        P(FS, TP),
        P(TP, FS),
        P(),
        P(),
        P(),
        P(),
        P(),
    )
    return jax.shard_map(body, mesh=fine, in_specs=placed, out_specs=P(FS, TP), check_vma=False)
```

```python
import functools
import math

import jax
import jax.numpy as jnp
from jax import lax
from jax.experimental import pallas as pl
from jax.experimental.pallas import tpu as pltpu
from jax.sharding import Mesh
from jax.sharding import PartitionSpec as P

D = 7168
TOK = 384
SLAB = 448
OUTW = 896
NEG = -1e30
BF = jnp.bfloat16
F32 = jnp.float32
FS = ("x_hi", "z", "core")
TP = ("x_lo", "y")
VM = pltpu.MemorySpace.VMEM
SM = pltpu.MemorySpace.SMEM
REL = ((0, 0), (0, 3), (0, 1), (1, 0), (1, 3), (0, 2), (1, 1), (1, 2))
NT = (((1,), (1,)), ((), ()))


def params(mib):
    return pltpu.CompilerParams(vmem_limit_bytes=mib << 20)


def cost(flops, nbytes, trans=0):
    return pl.CostEstimate(flops=flops, bytes_accessed=nbytes, transcendentals=trans)


def fsdp_pos():
    return (lax.axis_index("x_hi") * 4 + lax.axis_index("z")) * 2 + lax.axis_index("core")


def tp_pos():
    return lax.axis_index("x_lo") * 4 + lax.axis_index("y")


def fsdp_of(rel, other_core):
    dx, dz = rel
    hi = lax.axis_index("x_hi")
    core = lax.axis_index("core")
    hi = 1 - hi if dx else hi
    core = 1 - core if other_core else core
    return (hi * 4 + lax.rem(lax.axis_index("z") + dz, 4)) * 2 + core


def tp_of(rel):
    dx, dy = rel
    lo = lax.axis_index("x_lo")
    lo = 1 - lo if dx else lo
    return lo * 4 + lax.rem(lax.axis_index("y") + dy, 4)


def shift(x, axis, by):
    return lax.ppermute(x, axis, [(i, (i + by) % 4) for i in range(4)])


def swap(x, axis):
    return lax.ppermute(x, axis, [(0, 1), (1, 0)])


def scale_kernel(*refs):
    sources, outs, held, sems = refs[:9], refs[9:11], refs[11:20], refs[20]
    copies = [pltpu.make_async_copy(src, dst, sems.at[i]) for i, (src, dst) in enumerate(zip(sources, held))]
    for copy in copies:
        copy.start()
    for copy in copies:
        copy.wait()
    owner, eq, ek, ev, eo, wq, wk, wv, wo = held
    joined, send = outs
    slab = owner[fsdp_pos()]
    t = tp_pos()
    core = lax.axis_index("core")

    def factor(e):
        return jnp.where(e > 0, 2.0, jnp.where(e < 0, 0.5, 1.0)).astype(F32)

    def scaled(x, e):
        return (x.astype(F32) * factor(e)).astype(BF)

    for which in range(2):
        for mine in (True, False):

            @pl.when((core == which) == mine)
            def _():
                out = joined if mine else send
                top = which * SLAB if mine else 0
                w, e = ((wk, ek), (wv, ev))[which]
                for j in range(7):
                    rows = slice(j * 64, (j + 1) * 64)
                    to = slice(top + j * 64, top + (j + 1) * 64)
                    block = (slab * 7 + j) // 2
                    out[to, 0:128] = scaled(w[rows, :], e[t, block])
                    for i in range(2):
                        h = 2 * which + i
                        x = wq[rows, h * 128 : (h + 1) * 128]
                        out[to, (i + 1) * 128 : (i + 2) * 128] = scaled(x, eq[t * 4 + h, block])

    for j in range(7):
        rows = slice(j * 64, (j + 1) * 64)
        block = (slab * 7 + j) // 2
        for h in range(4):
            x = wo[rows, h * 128 : (h + 1) * 128]
            at = h // 2 * SLAB + j * 64
            joined[at : at + 64, 384 + h % 2 * 128 : 384 + (h % 2 + 1) * 128] = scaled(x, eo[t * 4 + h, block])


def scale(*operands):
    ints, floats = operands[:5], operands[5:]
    return pl.pallas_call(
        scale_kernel,
        in_specs=[pl.BlockSpec(memory_space=pl.ANY)] * 9,
        out_specs=[pl.BlockSpec(memory_space=VM)] * 2,
        out_shape=[
            jax.ShapeDtypeStruct((2 * SLAB, 640), BF),
            jax.ShapeDtypeStruct((SLAB, 384), BF),
        ],
        scratch_shapes=[
            *[pltpu.SMEM(x.shape, jnp.int32) for x in ints],
            *[pltpu.VMEM(x.shape, BF) for x in floats],
            pltpu.SemaphoreType.DMA((9,)),
        ],
        compiler_params=params(56),
        cost_estimate=cost(1 << 20, 3 << 20),
        name="scale",
    )(*operands)


def join_kernel(got, joined, out):
    at = pl.multiple_of((1 - lax.axis_index("core")) * SLAB, 64)
    out[pl.ds(at, SLAB), 0:384] = got[...]


def join(got, joined):
    return pl.pallas_call(
        join_kernel,
        in_specs=[pl.BlockSpec(memory_space=VM)] * 2,
        out_specs=pl.BlockSpec(memory_space=VM),
        out_shape=jax.ShapeDtypeStruct(joined.shape, BF),
        input_output_aliases={1: 0},
        compiler_params=params(8),
        cost_estimate=cost(0, 1 << 20),
        name="join",
    )(got, joined)


def arrange_kernel(owner, hid, waited, out):
    for p in range(0, 16, 2):
        halves = []
        chip = fsdp_of(REL[p // 2], False) // 2
        for i in range(2):
            slab = owner[chip * 2 + i]
            odd = lax.rem(slab, 2)
            window = hid[:, pl.ds(pl.multiple_of(slab * SLAB - odd * 64, 128), 512)]
            halves.append(jnp.where(odd == 1, window[:, 64:512], window[:, 0:448]))
        out[:, p * SLAB : (p + 2) * SLAB] = jnp.concatenate(halves, axis=1)


def arrange(owner, hidden, waited):
    return pl.pallas_call(
        arrange_kernel,
        in_specs=[pl.BlockSpec(memory_space=m) for m in (SM, VM, pl.ANY)],
        out_specs=pl.BlockSpec(memory_space=VM),
        out_shape=jax.ShapeDtypeStruct((TOK, D), BF),
        compiler_params=params(16),
        cost_estimate=cost(0, 4 * TOK * D),
        name="arrange",
    )(owner, hidden, waited)


def proj_kernel(at0, n, last, own, other, *refs):
    pieces, rest = refs[:n], refs[n:]
    core = lax.axis_index("core")
    for i, hid in enumerate((own, other)):
        part, at = rest[0][i] if at0 else None, at0
        for piece in pieces:
            rows = piece.shape[0]
            term = jnp.dot(hid[:, at : at + rows], piece[:, 0:384], preferred_element_type=F32)
            part = term if part is None else part + term
            at += rows
        if not last:
            rest[-1][i] = part
            continue
        kv = rest[1]
        slot = core if i == 0 else 1 - core
        kv[pl.ds(pl.multiple_of(slot * TOK, TOK), TOK), :] = part[:, 0:128].astype(BF)
        rest[2 + i][...] = (part[:, 128:384] * (math.log2(math.e) / math.sqrt(128))).astype(BF)


def proj(own, other, pieces, at0, before, name):
    rows = sum(p.shape[0] for p in pieces)
    last = at0 + rows == D
    operands = [own, other, *pieces, *before]
    shapes = [((2 * TOK, 128), BF), ((TOK, 256), BF), ((TOK, 256), BF)] if last else [((2, TOK, 384), F32)]
    return pl.pallas_call(
        functools.partial(proj_kernel, at0, len(pieces), last),
        in_specs=[pl.BlockSpec(memory_space=VM)] * len(operands),
        out_specs=[pl.BlockSpec(memory_space=VM)] * len(shapes),
        out_shape=[jax.ShapeDtypeStruct(*shape) for shape in shapes],
        compiler_params=params(16),
        cost_estimate=cost(4 * TOK * rows * 384, 2 * rows * (384 + 2 * TOK)),
        name=name,
    )(*operands)


def attend_kernel(n, q_here, q_there, *refs):
    parts, (out, kv, top, acc, sems) = refs[: 2 * n], refs[2 * n :]
    core = lax.axis_index("core")
    chip = lax.axis_index("x_hi") * 4 + lax.axis_index("z")
    copies = []
    for whose, slot in ((0, core), (1, 1 - core)):
        at = 0
        for i in range(whose * n, whose * n + n):
            rows = parts[i].shape[0]
            copies.append(pltpu.make_async_copy(parts[i], kv.at[slot, pl.ds(at, rows), :], sems.at[i]))
            copies[-1].start()
            at += rows
    for copy in copies:
        copy.wait()

    def scores(h, keys):
        q = (q_here, q_there)[h // 2][:, h % 2 * 128 : (h % 2 + 1) * 128]
        return lax.dot_general(q, keys, NT, preferred_element_type=F32)

    def step(at, width, first):
        keys = kv[0, pl.ds(at, width), :]
        values = kv[1, pl.ds(at, width), :]
        values = jnp.concatenate([values, jnp.ones_like(values)], axis=1)
        following = scores(0, keys)
        for h in range(4):
            s = following
            if h < 3:
                following = scores(h + 1, keys)
            if first:
                row = lax.broadcasted_iota(jnp.int32, s.shape, 0)
                col = lax.broadcasted_iota(jnp.int32, s.shape, 1)
                s = jnp.where(row >= col, s, NEG)
                m = jnp.max(s, axis=1, keepdims=True)
            else:
                old = top[h]
                m = jnp.maximum(old, jnp.max(s, axis=1, keepdims=True))
            top[h] = m
            mixed = jnp.dot(jnp.exp2(s - m).astype(BF), values, preferred_element_type=F32)
            acc[h] = mixed if first else acc[h] * jnp.exp2(old - m) + mixed

    step(pl.multiple_of(core * TOK, TOK), TOK, True)

    @pl.when(core == 1)
    def _():
        step(0, TOK, False)

    def earlier(j, carry):
        dx = jnp.where(j // 4 == lax.axis_index("x_hi"), 0, 1)
        dz = lax.rem(lax.rem(j, 4) - lax.axis_index("z") + 4, 4)
        near = jnp.where(dz == 0, 0, jnp.where(dz == 3, 1, jnp.where(dz == 1, 2, 5)))
        far = jnp.where(dz == 0, 3, jnp.where(dz == 3, 4, jnp.where(dz == 1, 6, 7)))
        step(pl.multiple_of(jnp.where(dx == 0, near, far) * 2 * TOK, 2 * TOK), 2 * TOK, False)
        return carry

    lax.fori_loop(0, chip, earlier, 0)
    for h in range(4):
        half = core if h < 2 else 1 - core
        cols = pl.ds(pl.multiple_of(half * 256 + h % 2 * 128, 128), 128)
        out[:, cols] = (acc[h][:, 0:128] / acc[h][:, 128:256]).astype(BF)


def attend(q_here, q_there, mine, theirs):
    n = len(mine)
    return pl.pallas_call(
        functools.partial(attend_kernel, n),
        in_specs=[pl.BlockSpec(memory_space=VM)] * 2 + [pl.BlockSpec(memory_space=pl.ANY)] * (2 * n),
        out_specs=pl.BlockSpec(memory_space=VM),
        out_shape=jax.ShapeDtypeStruct((TOK, 512), BF),
        scratch_shapes=[
            pltpu.VMEM((2, 16 * TOK, 128), BF),
            pltpu.VMEM((4, TOK, 1), F32),
            pltpu.VMEM((4, TOK, 256), F32),
            pltpu.SemaphoreType.DMA((2 * n,)),
        ],
        compiler_params=params(24),
        cost_estimate=cost(4 * 4 * TOK * 6144 * 128, 4 << 20, 4 * TOK * 6144),
        name="attend",
    )(q_here, q_there, *mine, *theirs)


def out_kernel(dests, cuts, owner, ctx, mine, theirs, *refs):
    outs, (held, sems) = refs[:-2], refs[-2:]
    slabs = [owner[fsdp_of(REL[p % 8], p >= 8)] for p in range(16)]

    def load(p, i, half, k):
        src = (theirs if p >= 8 else mine).at[pl.ds(((p % 8) * 2 + k) * SLAB, SLAB), :]
        rows = pl.ds(pl.multiple_of(i * OUTW + half * SLAB, 64), SLAB)
        dst = held.at[rows, k * 256 : (k + 1) * 256]
        return pltpu.make_async_copy(src, dst, sems.at[(2 * i + half) * 2 + k])

    for i, dest in enumerate(dests):
        t = tp_of(dest)
        for p in range(16):

            @pl.when(slabs[p] // 2 == t)
            def _():
                for k in range(2):
                    load(p, i, lax.rem(slabs[p], 2), k).start()

    for i in range(len(dests)):
        for half in range(2):
            for k in range(2):
                load(0, i, half, k).wait()
        for c, (r0, r1) in enumerate(cuts):
            part = lax.dot_general(
                ctx[r0:r1, :], held[i * OUTW : (i + 1) * OUTW, :], NT, preferred_element_type=F32
            )
            outs[i * len(cuts) + c][...] = part.astype(BF)


def project_out(owner, ctx, weights, dests, name, cuts=((0, TOK),)):
    n = len(dests)
    return pl.pallas_call(
        functools.partial(out_kernel, dests, cuts),
        in_specs=[
            pl.BlockSpec(memory_space=SM),
            pl.BlockSpec(memory_space=VM),
            *[pl.BlockSpec(memory_space=pl.ANY)] * 2,
        ],
        out_specs=[pl.BlockSpec(memory_space=VM)] * (n * len(cuts)),
        out_shape=[jax.ShapeDtypeStruct((r1 - r0, OUTW), BF) for _ in range(n) for r0, r1 in cuts],
        scratch_shapes=[pltpu.VMEM((n * OUTW, 512), BF), pltpu.SemaphoreType.DMA((4 * n,))],
        compiler_params=params(24),
        cost_estimate=cost(2 * n * TOK * 512 * OUTW, n * (3 << 20)),
        name=name,
    )(owner, ctx, *weights)


def add_kernel(places, base, *refs):
    addends, out = refs[:-1], refs[-1]
    for first in range(0, TOK, 128):
        rows = slice(first, first + 128)
        value = base[rows, :].astype(F32)
        for ref, at in zip(addends, places):
            if at <= first and first + 128 <= at + ref.shape[0]:
                value += ref[first - at : first - at + 128, :].astype(F32)
        out[rows, :] = value.astype(BF)


def add(base, addends):
    return pl.pallas_call(
        functools.partial(add_kernel, tuple(at for _, at in addends)),
        in_specs=[pl.BlockSpec(memory_space=VM)] * (1 + len(addends)),
        out_specs=pl.BlockSpec(memory_space=VM),
        out_shape=jax.ShapeDtypeStruct(base.shape, BF),
        compiler_params=params(8),
        cost_estimate=cost(len(addends) << 19, 3 << 20),
        name="add",
    )(base, *[x for x, _ in addends])


def pack_kernel(col, *refs):
    *pieces, out, sems = refs
    copies, at = [], 0
    for i, piece in enumerate(pieces):
        rows = piece.shape[0]
        src = piece.at[:, col : col + out.shape[1]]
        copies.append(pltpu.make_async_copy(src, out.at[pl.ds(at, rows), :], sems.at[i]))
        copies[-1].start()
        at += rows
    for copy in copies:
        copy.wait()


def pack(pieces, name, col, cols):
    rows = sum(p.shape[0] for p in pieces)
    return pl.pallas_call(
        functools.partial(pack_kernel, col),
        in_specs=[pl.BlockSpec(memory_space=pl.ANY)] * len(pieces),
        out_specs=pl.BlockSpec(memory_space=pl.ANY),
        out_shape=jax.ShapeDtypeStruct((rows, cols), BF),
        scratch_shapes=[pltpu.SemaphoreType.DMA((len(pieces),))],
        compiler_params=params(8),
        cost_estimate=cost(0, 4 * rows * cols),
        name=name,
    )(*pieces)


def gate_kernel(*refs):
    pass


def gate(waited, carry, name):
    n, every = len(waited), (*waited, *carry)
    return pl.pallas_call(
        gate_kernel,
        in_specs=[pl.BlockSpec(memory_space=pl.ANY)] * len(every),
        out_specs=[pl.BlockSpec(memory_space=pl.ANY)] * len(carry),
        out_shape=[jax.ShapeDtypeStruct(x.shape, x.dtype) for x in carry],
        input_output_aliases={n + i: i for i in range(len(carry))},
        compiler_params=params(1),
        cost_estimate=cost(0, 1024),
        name=name,
    )(*every)


def direct(own):
    pieces = []
    for dx, dz in REL[1:]:
        pairs = [(((h ^ dx) * 4 + (z + dz) % 4), h * 4 + z) for h in range(2) for z in range(4)]
        pieces.append(lax.ppermute(own, ("x_hi", "z"), pairs))
    return pieces


def first_stage(own):
    return shift(own, "z", 1), shift(own, "z", -1), swap(own, "x_hi")


def second_stage(a1, a2, a3):
    return shift(a3, "z", 1), shift(a2, "z", -1), swap(a2, "x_hi")


def third_stage(b1, b2, b3):
    rows = b1.shape[0]
    unit = 128 if rows % 128 == 0 else 16
    t1 = -(-rows // (3 * unit)) * unit
    t2 = t1 + -(-(rows - t1) // (2 * unit)) * unit
    return shift(b1[:t1], "z", 1), shift(b3[t1:t2], "z", -1), swap(b2[t2:], "x_hi")


def body(hidden, w_query, w_key, w_value, w_out, exp_query, exp_key, exp_value, exp_out, owner):
    there = swap(hidden, "core")
    joined, send = scale(
        owner, exp_query.T, exp_key.T, exp_value.T, exp_out, w_query, w_key, w_value, w_out.T
    )
    w_in = join(swap(send, "core"), joined)

    own, other = arrange(owner, hidden, w_in), arrange(owner, there, w_in)
    wa = gate([], first_stage(w_in), "gate_wa")
    wb = second_stage(*wa)
    sums = proj(own, other, [w_in, *wa], 0, (), "proj_a")
    wb = gate(sums, wb, "gate_wb")
    wc = third_stage(*wb)
    sums = proj(own, other, wb, 4 * 2 * SLAB, sums, "proj_b")
    wc = gate(sums, wc, "gate_wc")
    kv_here, q_here, q_send = proj(own, other, wc, 7 * 2 * SLAB, sums, "proj_c")

    va = first_stage(kv_here)
    o_mine = pack([w_in, *wa, *wb, *wc], "pack_wo", 384, 256)
    va = gate([o_mine], va, "gate_va")
    vb = second_stage(*va)
    q_there = swap(q_send, "core")
    o_theirs = swap(o_mine, "core")
    near = pack([kv_here, *va], "pack_near", 0, 128)
    vb = gate([q_there, o_theirs, near], vb, "gate_vb")
    vc = third_stage(*vb)
    middle = pack(vb, "pack_middle", 0, 128)
    mine = [near, middle, pack(vc, "pack_far", 0, 128)]
    theirs = [swap(x, "core") for x in mine]
    ctx = attend(q_here, q_there, mine, theirs)
    weights = (o_mine, o_theirs)

    out = functools.partial(project_out, owner, ctx, weights)
    p1, p2, p3 = out(((1, 2),), "out_far", cuts=((0, 128), (128, 256), (256, 384)))
    r1, r2, r3 = shift(p1, "y", -1), shift(p2, "y", 1), swap(p3, "x_lo")
    s1, s2, s3 = out(((1, 3), (0, 2), (1, 1)), "out_mid")
    s1, s2, s3 = add(s1, [(r1, 0)]), add(s2, [(r3, 256)]), add(s3, [(r2, 128)])
    u1, u2, u3 = shift(s1, "y", -1), shift(s2, "y", 1), swap(s3, "x_lo")
    v1, v2, v3, own = out(((0, 3), (0, 1), (1, 0), (0, 0)), "out_near")
    v2, v3 = add(v2, [(u2, 0), (u3, 0)]), add(v3, [(u1, 0)])
    g1, g2, g3 = shift(v1, "y", -1), shift(v2, "y", 1), swap(v3, "x_lo")
    return add(own, [(g1, 0), (g2, 0), (g3, 0)])


def solution(mesh):
    fine = Mesh(mesh.devices.reshape(2, 4, 2, 2, 4), ("x_hi", "z", "core", "x_lo", "y"))
    placed = (
        P(FS, None),
        P(FS, TP),
        P(FS, TP),
        P(FS, TP),
        P(TP, FS),
        P(),
        P(),
        P(),
        P(),
        P(),
    )
    return jax.shard_map(body, mesh=fine, in_specs=placed, out_specs=P(FS, TP), check_vma=False)
```

```python
import functools
import math

import jax
import jax.numpy as jnp
from jax import lax
from jax.experimental import pallas as pl
from jax.experimental.pallas import tpu as pltpu
from jax.sharding import Mesh
from jax.sharding import PartitionSpec as P

D = 7168
TOK = 384
SLAB = 448
OUTW = 896
NEG = -1e30
BF = jnp.bfloat16
F32 = jnp.float32
FS = ("x_hi", "z", "core")
TP = ("x_lo", "y")
VM = pltpu.MemorySpace.VMEM
SM = pltpu.MemorySpace.SMEM
REL = ((0, 0), (0, 3), (0, 1), (1, 0), (1, 3), (0, 2), (1, 1), (1, 2))
NT = (((1,), (1,)), ((), ()))


def params(mib):
    return pltpu.CompilerParams(vmem_limit_bytes=mib << 20)


def cost(flops, nbytes, trans=0):
    return pl.CostEstimate(flops=flops, bytes_accessed=nbytes, transcendentals=trans)


def fsdp_pos():
    return (lax.axis_index("x_hi") * 4 + lax.axis_index("z")) * 2 + lax.axis_index("core")


def tp_pos():
    return lax.axis_index("x_lo") * 4 + lax.axis_index("y")


def fsdp_of(rel, other_core):
    dx, dz = rel
    hi = lax.axis_index("x_hi")
    core = lax.axis_index("core")
    hi = 1 - hi if dx else hi
    core = 1 - core if other_core else core
    return (hi * 4 + lax.rem(lax.axis_index("z") + dz, 4)) * 2 + core


def tp_of(rel):
    dx, dy = rel
    lo = lax.axis_index("x_lo")
    lo = 1 - lo if dx else lo
    return lo * 4 + lax.rem(lax.axis_index("y") + dy, 4)


def shift(x, axis, by):
    return lax.ppermute(x, axis, [(i, (i + by) % 4) for i in range(4)])


def swap(x, axis):
    return lax.ppermute(x, axis, [(0, 1), (1, 0)])


def scale_kernel(*refs):
    sources, outs, held, sems = refs[:9], refs[9:11], refs[11:20], refs[20]
    copies = [pltpu.make_async_copy(src, dst, sems.at[i]) for i, (src, dst) in enumerate(zip(sources, held))]
    for copy in copies:
        copy.start()
    for copy in copies:
        copy.wait()
    owner, eq, ek, ev, eo, wq, wk, wv, wo = held
    joined, send = outs
    slab = owner[fsdp_pos()]
    t = tp_pos()
    core = lax.axis_index("core")

    def factor(e):
        return jnp.where(e > 0, 2.0, jnp.where(e < 0, 0.5, 1.0)).astype(F32)

    def scaled(x, e):
        return (x.astype(F32) * factor(e)).astype(BF)

    for which in range(2):
        for mine in (True, False):

            @pl.when((core == which) == mine)
            def _():
                out = joined if mine else send
                top = which * SLAB if mine else 0
                w, e = ((wk, ek), (wv, ev))[which]
                for j in range(7):
                    rows = slice(j * 64, (j + 1) * 64)
                    to = slice(top + j * 64, top + (j + 1) * 64)
                    block = (slab * 7 + j) // 2
                    out[to, 0:128] = scaled(w[rows, :], e[t, block])
                    for i in range(2):
                        h = 2 * which + i
                        x = wq[rows, h * 128 : (h + 1) * 128]
                        out[to, (i + 1) * 128 : (i + 2) * 128] = scaled(x, eq[t * 4 + h, block])

    for j in range(7):
        rows = slice(j * 64, (j + 1) * 64)
        block = (slab * 7 + j) // 2
        for h in range(4):
            x = wo[rows, h * 128 : (h + 1) * 128]
            at = h // 2 * SLAB + j * 64
            joined[at : at + 64, 384 + h % 2 * 128 : 384 + (h % 2 + 1) * 128] = scaled(x, eo[t * 4 + h, block])


def scale(*operands):
    ints, floats = operands[:5], operands[5:]
    return pl.pallas_call(
        scale_kernel,
        in_specs=[pl.BlockSpec(memory_space=pl.ANY)] * 9,
        out_specs=[pl.BlockSpec(memory_space=VM)] * 2,
        out_shape=[
            jax.ShapeDtypeStruct((2 * SLAB, 640), BF),
            jax.ShapeDtypeStruct((SLAB, 384), BF),
        ],
        scratch_shapes=[
            *[pltpu.SMEM(x.shape, jnp.int32) for x in ints],
            *[pltpu.VMEM(x.shape, BF) for x in floats],
            pltpu.SemaphoreType.DMA((9,)),
        ],
        compiler_params=params(56),
        cost_estimate=cost(1 << 20, 3 << 20),
        name="scale",
    )(*operands)


def join_kernel(got, joined, out):
    at = pl.multiple_of((1 - lax.axis_index("core")) * SLAB, 64)
    out[pl.ds(at, SLAB), 0:384] = got[...]


def join(got, joined):
    return pl.pallas_call(
        join_kernel,
        in_specs=[pl.BlockSpec(memory_space=VM)] * 2,
        out_specs=pl.BlockSpec(memory_space=VM),
        out_shape=jax.ShapeDtypeStruct(joined.shape, BF),
        input_output_aliases={1: 0},
        compiler_params=params(8),
        cost_estimate=cost(0, 1 << 20),
        name="join",
    )(got, joined)


def arrange_kernel(owner, hid, waited, out):
    for p in range(0, 16, 2):
        halves = []
        chip = fsdp_of(REL[p // 2], False) // 2
        for i in range(2):
            slab = owner[chip * 2 + i]
            odd = lax.rem(slab, 2)
            window = hid[:, pl.ds(pl.multiple_of(slab * SLAB - odd * 64, 128), 512)]
            halves.append(jnp.where(odd == 1, window[:, 64:512], window[:, 0:448]))
        out[:, p * SLAB : (p + 2) * SLAB] = jnp.concatenate(halves, axis=1)


def arrange(owner, hidden, waited):
    return pl.pallas_call(
        arrange_kernel,
        in_specs=[pl.BlockSpec(memory_space=m) for m in (SM, VM, pl.ANY)],
        out_specs=pl.BlockSpec(memory_space=VM),
        out_shape=jax.ShapeDtypeStruct((TOK, D), BF),
        compiler_params=params(16),
        cost_estimate=cost(0, 4 * TOK * D),
        name="arrange",
    )(owner, hidden, waited)


def proj_kernel(at0, n, last, own, other, *refs):
    pieces, rest = refs[:n], refs[n:]
    core = lax.axis_index("core")
    for i, hid in enumerate((own, other)):
        part, at = rest[0][i] if at0 else None, at0
        for piece in pieces:
            rows = piece.shape[0]
            term = jnp.dot(hid[:, at : at + rows], piece[:, 0:384], preferred_element_type=F32)
            part = term if part is None else part + term
            at += rows
        if not last:
            rest[-1][i] = part
            continue
        kv = rest[1]
        slot = core if i == 0 else 1 - core
        kv[pl.ds(pl.multiple_of(slot * TOK, TOK), TOK), :] = part[:, 0:128].astype(BF)
        rest[2 + i][...] = (part[:, 128:384] * (math.log2(math.e) / math.sqrt(128))).astype(BF)


def proj(own, other, pieces, at0, before, name):
    rows = sum(p.shape[0] for p in pieces)
    last = at0 + rows == D
    operands = [own, other, *pieces, *before]
    shapes = [((2 * TOK, 128), BF), ((TOK, 256), BF), ((TOK, 256), BF)] if last else [((2, TOK, 384), F32)]
    return pl.pallas_call(
        functools.partial(proj_kernel, at0, len(pieces), last),
        in_specs=[pl.BlockSpec(memory_space=VM)] * len(operands),
        out_specs=[pl.BlockSpec(memory_space=VM)] * len(shapes),
        out_shape=[jax.ShapeDtypeStruct(*shape) for shape in shapes],
        compiler_params=params(16),
        cost_estimate=cost(4 * TOK * rows * 384, 2 * rows * (384 + 2 * TOK)),
        name=name,
    )(*operands)


def attend_kernel(n, q_here, q_there, *refs):
    parts, (out, kv, top, acc, sems) = refs[: 2 * n], refs[2 * n :]
    core = lax.axis_index("core")
    chip = lax.axis_index("x_hi") * 4 + lax.axis_index("z")
    copies = []
    for whose, slot in ((0, core), (1, 1 - core)):
        at = 0
        for i in range(whose * n, whose * n + n):
            rows = parts[i].shape[0]
            copies.append(pltpu.make_async_copy(parts[i], kv.at[slot, pl.ds(at, rows), :], sems.at[i]))
            copies[-1].start()
            at += rows
    for copy in copies:
        copy.wait()

    def scores(h, keys):
        q = (q_here, q_there)[h // 2][:, h % 2 * 128 : (h % 2 + 1) * 128]
        return lax.dot_general(q, keys, NT, preferred_element_type=F32)

    def step(at, width, first):
        keys = kv[0, pl.ds(at, width), :]
        values = kv[1, pl.ds(at, width), :]
        values = jnp.concatenate([values, jnp.ones_like(values)], axis=1)
        following = scores(0, keys)
        for h in range(4):
            s = following
            if h < 3:
                following = scores(h + 1, keys)
            if first:
                row = lax.broadcasted_iota(jnp.int32, s.shape, 0)
                col = lax.broadcasted_iota(jnp.int32, s.shape, 1)
                s = jnp.where(row >= col, s, NEG)
                m = jnp.max(s, axis=1, keepdims=True)
            else:
                old = top[h]
                m = jnp.maximum(old, jnp.max(s, axis=1, keepdims=True))
            top[h] = m
            mixed = jnp.dot(jnp.exp2(s - m).astype(BF), values, preferred_element_type=F32)
            acc[h] = mixed if first else acc[h] * jnp.exp2(old - m) + mixed

    step(pl.multiple_of(core * TOK, TOK), TOK, True)

    @pl.when(core == 1)
    def _():
        step(0, TOK, False)

    def earlier(j, carry):
        dx = jnp.where(j // 4 == lax.axis_index("x_hi"), 0, 1)
        dz = lax.rem(lax.rem(j, 4) - lax.axis_index("z") + 4, 4)
        near = jnp.where(dz == 0, 0, jnp.where(dz == 3, 1, jnp.where(dz == 1, 2, 5)))
        far = jnp.where(dz == 0, 3, jnp.where(dz == 3, 4, jnp.where(dz == 1, 6, 7)))
        step(pl.multiple_of(jnp.where(dx == 0, near, far) * 2 * TOK, 2 * TOK), 2 * TOK, False)
        return carry

    lax.fori_loop(0, chip, earlier, 0)
    for h in range(4):
        half = core if h < 2 else 1 - core
        cols = pl.ds(pl.multiple_of(half * 256 + h % 2 * 128, 128), 128)
        out[:, cols] = (acc[h][:, 0:128] / acc[h][:, 128:256]).astype(BF)


def attend(q_here, q_there, mine, theirs):
    n = len(mine)
    return pl.pallas_call(
        functools.partial(attend_kernel, n),
        in_specs=[pl.BlockSpec(memory_space=VM)] * 2 + [pl.BlockSpec(memory_space=pl.ANY)] * (2 * n),
        out_specs=pl.BlockSpec(memory_space=VM),
        out_shape=jax.ShapeDtypeStruct((TOK, 512), BF),
        scratch_shapes=[
            pltpu.VMEM((2, 16 * TOK, 128), BF),
            pltpu.VMEM((4, TOK, 1), F32),
            pltpu.VMEM((4, TOK, 256), F32),
            pltpu.SemaphoreType.DMA((2 * n,)),
        ],
        compiler_params=params(24),
        cost_estimate=cost(4 * 4 * TOK * 6144 * 128, 4 << 20, 4 * TOK * 6144),
        name="attend",
    )(q_here, q_there, *mine, *theirs)


def out_kernel(dests, cuts, owner, ctx, mine, theirs, *refs):
    outs, (held, sems) = refs[:-2], refs[-2:]
    slabs = [owner[fsdp_of(REL[p % 8], p >= 8)] for p in range(16)]

    def load(p, i, half, k):
        src = (theirs if p >= 8 else mine).at[pl.ds(((p % 8) * 2 + k) * SLAB, SLAB), :]
        rows = pl.ds(pl.multiple_of(i * OUTW + half * SLAB, 64), SLAB)
        dst = held.at[rows, k * 256 : (k + 1) * 256]
        return pltpu.make_async_copy(src, dst, sems.at[(2 * i + half) * 2 + k])

    for i, dest in enumerate(dests):
        t = tp_of(dest)
        for p in range(16):

            @pl.when(slabs[p] // 2 == t)
            def _():
                for k in range(2):
                    load(p, i, lax.rem(slabs[p], 2), k).start()

    for i in range(len(dests)):
        for half in range(2):
            for k in range(2):
                load(0, i, half, k).wait()
        for c, (r0, r1) in enumerate(cuts):
            part = lax.dot_general(
                ctx[r0:r1, :], held[i * OUTW : (i + 1) * OUTW, :], NT, preferred_element_type=F32
            )
            outs[i * len(cuts) + c][...] = part.astype(BF)


def project_out(owner, ctx, weights, dests, name, cuts=((0, TOK),)):
    n = len(dests)
    return pl.pallas_call(
        functools.partial(out_kernel, dests, cuts),
        in_specs=[
            pl.BlockSpec(memory_space=SM),
            pl.BlockSpec(memory_space=VM),
            *[pl.BlockSpec(memory_space=pl.ANY)] * 2,
        ],
        out_specs=[pl.BlockSpec(memory_space=VM)] * (n * len(cuts)),
        out_shape=[jax.ShapeDtypeStruct((r1 - r0, OUTW), BF) for _ in range(n) for r0, r1 in cuts],
        scratch_shapes=[pltpu.VMEM((n * OUTW, 512), BF), pltpu.SemaphoreType.DMA((4 * n,))],
        compiler_params=params(24),
        cost_estimate=cost(2 * n * TOK * 512 * OUTW, n * (3 << 20)),
        name=name,
    )(owner, ctx, *weights)


def add_kernel(places, base, *refs):
    addends, out = refs[:-1], refs[-1]
    for first in range(0, TOK, 128):
        rows = slice(first, first + 128)
        value = base[rows, :].astype(F32)
        for ref, at in zip(addends, places):
            if at <= first and first + 128 <= at + ref.shape[0]:
                value += ref[first - at : first - at + 128, :].astype(F32)
        out[rows, :] = value.astype(BF)


def add(base, addends):
    return pl.pallas_call(
        functools.partial(add_kernel, tuple(at for _, at in addends)),
        in_specs=[pl.BlockSpec(memory_space=VM)] * (1 + len(addends)),
        out_specs=pl.BlockSpec(memory_space=VM),
        out_shape=jax.ShapeDtypeStruct(base.shape, BF),
        compiler_params=params(8),
        cost_estimate=cost(len(addends) << 19, 3 << 20),
        name="add",
    )(base, *[x for x, _ in addends])


def pack_kernel(col, *refs):
    *pieces, out, sems = refs
    copies, at = [], 0
    for i, piece in enumerate(pieces):
        rows = piece.shape[0]
        src = piece.at[:, col : col + out.shape[1]]
        copies.append(pltpu.make_async_copy(src, out.at[pl.ds(at, rows), :], sems.at[i]))
        copies[-1].start()
        at += rows
    for copy in copies:
        copy.wait()


def pack(pieces, name, col, cols):
    rows = sum(p.shape[0] for p in pieces)
    return pl.pallas_call(
        functools.partial(pack_kernel, col),
        in_specs=[pl.BlockSpec(memory_space=pl.ANY)] * len(pieces),
        out_specs=pl.BlockSpec(memory_space=pl.ANY),
        out_shape=jax.ShapeDtypeStruct((rows, cols), BF),
        scratch_shapes=[pltpu.SemaphoreType.DMA((len(pieces),))],
        compiler_params=params(8),
        cost_estimate=cost(0, 4 * rows * cols),
        name=name,
    )(*pieces)


def gate_kernel(*refs):
    pass


def gate(waited, carry, name):
    n, every = len(waited), (*waited, *carry)
    return pl.pallas_call(
        gate_kernel,
        in_specs=[pl.BlockSpec(memory_space=pl.ANY)] * len(every),
        out_specs=[pl.BlockSpec(memory_space=pl.ANY)] * len(carry),
        out_shape=[jax.ShapeDtypeStruct(x.shape, x.dtype) for x in carry],
        input_output_aliases={n + i: i for i in range(len(carry))},
        compiler_params=params(1),
        cost_estimate=cost(0, 1024),
        name=name,
    )(*every)


def direct(own):
    pieces = []
    for dx, dz in REL[1:]:
        pairs = [(((h ^ dx) * 4 + (z + dz) % 4), h * 4 + z) for h in range(2) for z in range(4)]
        pieces.append(lax.ppermute(own, ("x_hi", "z"), pairs))
    return pieces


def first_stage(own):
    return shift(own, "z", 1), shift(own, "z", -1), swap(own, "x_hi")


def second_stage(a1, a2, a3):
    return shift(a3, "z", 1), shift(a2, "z", -1), swap(a2, "x_hi")


def third_stage(b1, b2, b3):
    rows = b1.shape[0]
    unit = 128 if rows % 128 == 0 else 16
    t1 = -(-rows // (3 * unit)) * unit
    t2 = t1 + -(-(rows - t1) // (2 * unit)) * unit
    return shift(b1[:t1], "z", 1), shift(b3[t1:t2], "z", -1), swap(b2[t2:], "x_hi")


def body(hidden, w_query, w_key, w_value, w_out, exp_query, exp_key, exp_value, exp_out, owner):
    joined, send = scale(
        owner, exp_query.T, exp_key.T, exp_value.T, exp_out, w_query, w_key, w_value, w_out.T
    )
    (w_in,) = [join(swap(send, "core"), joined)]

    later, w_in = lax.optimization_barrier((hidden, w_in))
    there = swap(later, "core")
    wa = gate([], first_stage(w_in), "gate_wa")
    own, other = arrange(owner, hidden, wa[0]), arrange(owner, there, wa[0])
    wb = second_stage(*wa)
    sums = proj(own, other, [w_in, *wa], 0, (), "proj_a")
    wb = gate(sums, wb, "gate_wb")
    wc = third_stage(*wb)
    sums = proj(own, other, wb, 4 * 2 * SLAB, sums, "proj_b")
    wc = gate(sums, wc, "gate_wc")
    kv_here, q_here, q_send = proj(own, other, wc, 7 * 2 * SLAB, sums, "proj_c")

    va = first_stage(kv_here)
    o_mine = pack([w_in, *wa, *wb, *wc], "pack_wo", 384, 256)
    va = gate([o_mine], va, "gate_va")
    vb = second_stage(*va)
    q_there = swap(q_send, "core")
    o_theirs = swap(o_mine, "core")
    near = pack([kv_here, *va], "pack_near", 0, 128)
    vb = gate([q_there, o_theirs, near], vb, "gate_vb")
    vc = third_stage(*vb)
    middle = pack(vb, "pack_middle", 0, 128)
    mine = [near, middle, pack(vc, "pack_far", 0, 128)]
    theirs = [swap(x, "core") for x in mine]
    ctx = attend(q_here, q_there, mine, theirs)
    weights = (o_mine, o_theirs)

    out = functools.partial(project_out, owner, ctx, weights)
    p1, p2, p3 = out(((1, 2),), "out_far", cuts=((0, 128), (128, 256), (256, 384)))
    r1, r2, r3 = shift(p1, "y", -1), shift(p2, "y", 1), swap(p3, "x_lo")
    s1, s2, s3 = out(((1, 3), (0, 2), (1, 1)), "out_mid")
    s1, s2, s3 = add(s1, [(r1, 0)]), add(s2, [(r3, 256)]), add(s3, [(r2, 128)])
    u1, u2, u3 = shift(s1, "y", -1), shift(s2, "y", 1), swap(s3, "x_lo")
    v1, v2, v3, own = out(((0, 3), (0, 1), (1, 0), (0, 0)), "out_near")
    v2, v3 = add(v2, [(u2, 0), (u3, 0)]), add(v3, [(u1, 0)])
    g1, g2, g3 = shift(v1, "y", -1), shift(v2, "y", 1), swap(v3, "x_lo")
    return add(own, [(g1, 0), (g2, 0), (g3, 0)])


def solution(mesh):
    fine = Mesh(mesh.devices.reshape(2, 4, 2, 2, 4), ("x_hi", "z", "core", "x_lo", "y"))
    placed = (
        P(FS, None),
        P(FS, TP),
        P(FS, TP),
        P(FS, TP),
        P(TP, FS),
        P(),
        P(),
        P(),
        P(),
        P(),
    )
    return jax.shard_map(body, mesh=fine, in_specs=placed, out_specs=P(FS, TP), check_vma=False)
```
